32 devices in a mesh: ctx: 16 (over z, y, core), uly: 2 (over x).
Axes of the slice: x: 2, y: 2, z: 4, core: 2. Of those that a mesh axis runs over, the one named last changes fastest.
Arguments:
- queries: bfloat16 [4096, 4096], P(('ctx', 'uly')), may hold values from -200 to 200, as said below
- keys: bfloat16 [4096, 1024], P(('ctx', 'uly')), may hold values from -6 to 6, as said below
- values: bfloat16 [4096, 1024], P(('ctx', 'uly')), may hold values from -6 to 6
Outputs:
- attended: bfloat16 [4096, 4096], P(('ctx', 'uly'))
The draws below stay inside these ranges and needn't reach their ends.
Inputs may be any that keep to these rules, and one draw needn't show every extreme that they name: `queries`: entries of order one, except that some query rows may be large. `keys`: entries of order one.
All inputs are finite; a program needn't handle non-finite values.
Results may differ from the reference program's by a relative error of at most 0.0055.
Values may be sent and summed in bfloat16 or wider, within the bound.
A program may use at most 64 MiB of HBM per device.

```python
import jax
import jax.numpy as jnp
from jax import lax

HQ = 32
KEY_VALUE_HEADS = 8
HEAD_SIZE = 128
WINDOW_BLOCKS = 3
QUERY_PER_KEY = 4
BLOCK_TOKENS = 256
SEQUENCE_TOKENS = 4096
N_CTX = 16


def common_keys(key):
    base_offset = jax.random.normal(jax.random.fold_in(key, 11), (SEQUENCE_TOKENS, KEY_VALUE_HEADS * HEAD_SIZE), jnp.float32)
    base_offset = jnp.clip(base_offset, -4.5, 4.5)
    return base_offset


def draw_keys(key, part):
    return common_keys(key).astype(jnp.bfloat16)


def draw_queries(key, part):
    drawn_output = jax.random.normal(jax.random.fold_in(key, 12), (SEQUENCE_TOKENS, HQ * HEAD_SIZE), jnp.float32)
    drawn_output = jnp.clip(drawn_output, -4.5, 4.5)
    return drawn_output.astype(jnp.bfloat16)


def shard_levels(own_key, shape, split, low, largest):
    def one(dim, shards_of):
        steps = jax.random.uniform(jax.random.fold_in(jax.random.fold_in(own_key, 6), dim), (shards_of,), jnp.float32, low / len(split), largest / len(split))
        return jnp.repeat(jnp.exp(steps), shape[dim] // shards_of).reshape((-1,) + (1,) * (len(shape) - dim - 1))

    factor_of = one(*split[0])
    for cut in split[1:]:
        factor_of = factor_of * one(*cut)
    return factor_of


def scatter_about(stream_key, extent, spread, most, cuts=(), held_as=jnp.bfloat16):
    result = jax.random.normal(stream_key, extent, jnp.float32) * spread
    if len(cuts) > 0:
        result = shard_levels(stream_key, extent, cuts, -0.22, 0.18) * result
    return jnp.clip(result, min=-most, max=most).astype(held_as)


def setup_inputs(seed: int = 0) -> dict:
    arg_keys = jax.random.split(jax.random.key(seed), 4)
    return {
        "queries": draw_queries(jax.random.fold_in(arg_keys[3], 71), 0),
        "keys": draw_keys(jax.random.fold_in(arg_keys[3], 71), 0),
        "values": scatter_about(arg_keys[2], (SEQUENCE_TOKENS, KEY_VALUE_HEADS * HEAD_SIZE), 1.0, 6.0, ((0, 32),)),
    }


def reference(queries, keys, values):
    scale_factor = HEAD_SIZE ** -0.5
    window = (WINDOW_BLOCKS + 1) * BLOCK_TOKENS
    front_block = jnp.zeros((WINDOW_BLOCKS * BLOCK_TOKENS, KEY_VALUE_HEADS * HEAD_SIZE), jnp.bfloat16)
    padded_keys = jnp.concatenate([front_block, keys], axis=0).reshape(SEQUENCE_TOKENS + WINDOW_BLOCKS * BLOCK_TOKENS, KEY_VALUE_HEADS, HEAD_SIZE)
    padded_values = jnp.concatenate([front_block, values], axis=0).reshape(SEQUENCE_TOKENS + WINDOW_BLOCKS * BLOCK_TOKENS, KEY_VALUE_HEADS, HEAD_SIZE)
    query_lattice = queries.reshape(SEQUENCE_TOKENS, KEY_VALUE_HEADS, QUERY_PER_KEY, HEAD_SIZE)

    def single_entry(index_value):
        block_number = index_value // KEY_VALUE_HEADS
        key_value_index = index_value % KEY_VALUE_HEADS
        start = (block_number * BLOCK_TOKENS).astype(jnp.int32)
        zero_index = jnp.int32(0)
        query_part = lax.dynamic_slice(query_lattice, (start, key_value_index, zero_index, zero_index), (BLOCK_TOKENS, 1, QUERY_PER_KEY, HEAD_SIZE))[:, 0].astype(jnp.float32)
        key_part = lax.dynamic_slice(padded_keys, (start, key_value_index, zero_index), (window, 1, HEAD_SIZE))[:, 0].astype(jnp.float32)
        value_part = lax.dynamic_slice(padded_values, (start, key_value_index, zero_index), (window, 1, HEAD_SIZE))[:, 0].astype(jnp.float32)
        scores = jnp.einsum("qgd,td->gqt", query_part, key_part) * scale_factor
        query_pos = start + jnp.arange(BLOCK_TOKENS, dtype=jnp.int32)
        key_pos = start - WINDOW_BLOCKS * BLOCK_TOKENS + jnp.arange(window, dtype=jnp.int32)
        visible = (key_pos[None, :] >= 0) & (key_pos[None, :] <= query_pos[:, None])
        scores = jnp.where(visible[None], scores, jnp.float32(-1e30))
        highest = jnp.max(scores, axis=-1, keepdims=True)
        weights = jnp.where(visible[None], jnp.exp(scores - highest), jnp.float32(0.0))
        totals = jnp.sum(weights, axis=-1)
        rounded = lax.optimization_barrier(weights.astype(jnp.bfloat16)).astype(jnp.float32)
        mixed = jnp.einsum("gqt,td->gqd", rounded, value_part) / totals[..., None]
        return mixed.astype(jnp.bfloat16)

    output_list = lax.map(single_entry, jnp.arange(N_CTX * KEY_VALUE_HEADS, dtype=jnp.int32))
    output_list = output_list.reshape(N_CTX, KEY_VALUE_HEADS, QUERY_PER_KEY, BLOCK_TOKENS, HEAD_SIZE).transpose(0, 3, 1, 2, 4)
    return output_list.reshape(SEQUENCE_TOKENS, HQ * HEAD_SIZE)
```

```python
import functools

import jax
import jax.numpy as jnp
from jax import lax
from jax.experimental import pallas as pl
from jax.experimental.pallas import tpu as pltpu
from jax.sharding import PartitionSpec as P

HEAD_SIZE = 128
WINDOW_BLOCKS = 3


def passed_along(block, axis, distance):
    devices = range(lax.axis_size(axis))
    route = [(i - distance, i) for i in devices if i - distance in devices]
    return lax.ppermute(block, axis, route)


def on_device(queries, keys, values):
    scale_factor = HEAD_SIZE ** (-0.5)
    cycle_pos = lax.axis_index("ctx")
    query_here, key_here, value_here = (
        lax.all_to_all(queries, "uly", split_axis=1, concat_axis=0, tiled=True),
        lax.all_to_all(keys, "uly", split_axis=1, concat_axis=0, tiled=True),
        lax.all_to_all(values, "uly", split_axis=1, concat_axis=0, tiled=True),
    )
    block_len = query_here.shape[0]
    q_heads = query_here.shape[1] // HEAD_SIZE
    kv_heads = key_here.shape[1] // HEAD_SIZE
    group_size = q_heads // kv_heads
    row_block = min(block_len, 512)
    pieces = block_len // row_block
    item_count = q_heads * pieces
    query_items = (
        query_here.reshape(block_len, q_heads, HEAD_SIZE)
        .transpose(1, 0, 2)
        .reshape(item_count, row_block, HEAD_SIZE)
    )
    key_blocks = key_here.reshape(block_len, kv_heads, HEAD_SIZE).transpose(1, 0, 2)
    value_blocks = value_here.reshape(block_len, kv_heads, HEAD_SIZE).transpose(1, 0, 2)
    carry_state = (
        jnp.full((item_count, row_block), -1e30, jnp.float32),
        jnp.zeros((item_count, row_block), jnp.float32),
        jnp.zeros((item_count, row_block, HEAD_SIZE), jnp.float32),
    )

    def absorb(carry_state, key_set, value_set, step_back):

        def per_item(inputs):
            item_index, running_max, running_sum, weighted, query_rows = inputs
            key_value_index = item_index // (pieces * group_size)
            key_rows = lax.dynamic_index_in_dim(key_set, key_value_index, 0, keepdims=False)
            value_rows = lax.dynamic_index_in_dim(value_set, key_value_index, 0, keepdims=False)
            scores = (
                jnp.einsum("qd,td->qt", query_rows, key_rows, preferred_element_type=jnp.float32)
                * scale_factor
            )
            if step_back == 0:
                query_pos = item_index % pieces * row_block + jnp.arange(row_block, dtype=jnp.int32)
                key_pos = jnp.arange(block_len, dtype=jnp.int32)
                visible = key_pos[None, :] <= query_pos[:, None]
            else:
                visible = jnp.broadcast_to(cycle_pos >= step_back, scores.shape)
            scores = jnp.where(visible, scores, jnp.float32(-1e30))
            new_max = jnp.maximum(running_max, jnp.max(scores, axis=-1))
            weights = jnp.where(visible, jnp.exp(scores - new_max[:, None]), jnp.float32(0.0))
            factor = jnp.exp(running_max - new_max)
            new_sum = running_sum * factor + jnp.sum(weights, axis=-1)
            product = jnp.einsum(
                "qt,td->qd",
                weights.astype(jnp.bfloat16),
                value_rows,
                preferred_element_type=jnp.float32,
            )
            return (new_max, new_sum, weighted * factor[:, None] + product)

        return lax.map(
            per_item,
            (
                jnp.arange(item_count, dtype=jnp.int32),
                carry_state[0],
                carry_state[1],
                carry_state[2],
                query_items,
            ),
        )

    carry_state = absorb(carry_state, key_blocks, value_blocks, 0)
    current = (key_blocks, value_blocks)
    for step_back in range(1, WINDOW_BLOCKS + 1):
        current = passed_along((current[0], current[1]), "ctx", 1)
        carry_state = absorb(carry_state, current[0], current[1], step_back)
    output_rows = (carry_state[2] / carry_state[1][..., None]).astype(jnp.bfloat16)
    output_rows = (
        output_rows.reshape(q_heads, block_len, HEAD_SIZE)
        .transpose(1, 0, 2)
        .reshape(block_len, q_heads * HEAD_SIZE)
    )
    return lax.all_to_all(output_rows, "uly", split_axis=0, concat_axis=1, tiled=True)


MESH = pl.DeviceIdType.MESH
LOG2_E = 1.4426950408889634


def attention_kernel(
    pairs,
    groups,
    q_ref,
    k_ref,
    v_ref,
    out_ref,
    kv,
    q_here,
    o_here,
    own_sem,
    pair_send,
    slot_sem,
    send_sem,
    q_sem,
    o_sem,
):
    ctx = lax.axis_index("ctx")
    half = lax.axis_index("uly")
    other = 1 - half
    pair, core = ctx // 2, lax.rem(ctx, 2)
    odd = lax.rem(pair, 2)
    chunks = kv.shape[0]
    rows = q_ref.shape[0]
    q_cols = q_ref.shape[1] // 2
    wide = q_cols // chunks

    mate = (2 * pair + 1 - core, half)
    across = (ctx, other)
    ahead1, ahead2 = (ctx + 2, half), (ctx + 4, half)
    behind1, behind2 = (ctx - 2, half), (ctx - 4, half)
    has_a1, has_a2 = pair + 1 < pairs, pair + 2 < pairs
    has_b1, has_b2 = pair >= 1, pair >= 2
    even = odd == 0
    always = pair >= 0

    barrier = pltpu.get_barrier_semaphore()
    count = jnp.int32(0)
    for device, exists in (
        (mate, always),
        (across, always),
        (ahead1, has_a1),
        (ahead2, has_a2),
        (behind1, has_b1),
        (behind2, has_b2),
    ):
        count += exists.astype(jnp.int32)

        @pl.when(exists)
        def _():
            pl.semaphore_signal(barrier, inc=1, device_id=device, device_id_type=MESH)

    def column(ref, head):
        return ref.at[:, pl.ds(pl.multiple_of(head * HEAD_SIZE, HEAD_SIZE), HEAD_SIZE)]

    def q_part(ref, index):
        return ref.at[:, pl.ds(pl.multiple_of(index * q_cols, q_cols), q_cols)]

    own = []
    for chunk in range(chunks):
        for which, ref in enumerate((k_ref, v_ref)):
            copy = pltpu.make_async_copy(
                column(ref, core * chunks + chunk),
                kv.at[chunk, which, 1 - core, half],
                own_sem.at[chunk, 1 - core, which],
            )
            copy.start()
    q_own = pltpu.make_async_copy(q_part(q_ref, core), q_here.at[core], q_sem.at[0])
    q_own.start()

    @pl.when(pair < 2)
    def _():
        for d in (2, 3, 4):

            @pl.when(2 * pair + 1 - d < 0)
            def _():
                kv[:, :, d] = jnp.zeros_like(kv[:, :, d])

    pl.semaphore_wait(barrier, count)

    pending = []

    def send(src, dst, sent, landed, device, exists):
        copy = pltpu.make_async_remote_copy(
            src_ref=src, dst_ref=dst, send_sem=sent, recv_sem=landed, device_id=device, device_id_type=MESH
        )

        @pl.when(exists)
        def _():
            copy.start()

        pending.append((copy, exists))

    for chunk in range(chunks):
        for which, ref in enumerate((k_ref, v_ref)):
            send(
                column(ref, (1 - core) * chunks + chunk),
                kv.at[chunk, which, 1 - core, half],
                pair_send.at[chunk, which],
                own_sem.at[chunk, 1 - core, which],
                mate,
                always,
            )
    def await_own(chunk, d):
        for which in range(2):
            ref = kv.at[chunk, which, d, half]
            pltpu.make_async_copy(ref, ref, own_sem.at[chunk, d, which]).wait()

    def await_slot(chunk, d, side, exists=None):
        ref = kv.at[chunk, :, d, side]
        copy = pltpu.make_async_copy(ref, ref, slot_sem.at[chunk, d, side])
        if exists is None:
            copy.wait()
        else:

            @pl.when(exists)
            def _():
                copy.wait()

    def pass_on(chunk, src_d, dst_d, side, route, device, exists):
        send(
            kv.at[chunk, :, src_d, side],
            kv.at[chunk, :, dst_d, side],
            send_sem.at[chunk, route],
            slot_sem.at[chunk, dst_d, side],
            device,
            exists,
        )

    def origin(chunk):
        await_own(chunk, 0)
        pass_on(chunk, 0, 0, half, 0, across, always)
        pass_on(chunk, 0, 4, half, 1, ahead2, has_a2)
        pass_on(chunk, 0, 2, half, 2, ahead1, has_a1 & even)
        await_own(chunk, 1)
        pass_on(chunk, 1, 3, half, 3, ahead1, has_a1)
        pass_on(chunk, 1, 1, half, 4, across, always)

    def relay(chunk):
        await_slot(chunk, 0, other)
        pass_on(chunk, 0, 4, other, 5, ahead2, has_a2)
        pass_on(chunk, 0, 2, other, 6, ahead1, has_a1 & even)
        await_slot(chunk, 3, half, has_b1)
        pass_on(chunk, 3, 3, half, 7, across, has_b1)
        from_far = has_b2 & (odd == 1)
        await_slot(chunk, 4, half, from_far)
        pass_on(chunk, 4, 2, half, 8, behind1, from_far)
        await_slot(chunk, 4, other, from_far)
        pass_on(chunk, 4, 2, other, 9, behind1, from_far)

    def gather(chunk):
        await_slot(chunk, 1, other)
        await_slot(chunk, 4, half, has_b2 & even)
        await_slot(chunk, 4, other, has_b2 & even)
        await_slot(chunk, 3, other, has_b1)
        await_slot(chunk, 2, half, has_b1)
        await_slot(chunk, 2, other, has_b1)

    factor = HEAD_SIZE ** (-0.5) * LOG2_E
    keys = 8 * rows

    def attend(chunk):
        def body(index, _):
            side, head = index // groups, lax.rem(index, groups)
            first = 1 - side
            cols = pl.ds(pl.multiple_of(chunk * wide + head * HEAD_SIZE, HEAD_SIZE), HEAD_SIZE)
            query = q_here[side, :, cols]
            key = kv[chunk, 0, pl.ds(first, 4)].reshape(keys, HEAD_SIZE)
            value = kv[chunk, 1, pl.ds(first, 4)].reshape(keys, HEAD_SIZE)
            scores = lax.dot_general(
                query, key, (((1,), (1,)), ((), ())), preferred_element_type=jnp.float32
            )
            row = lax.broadcasted_iota(jnp.int32, (rows, keys), 0)
            col = lax.broadcasted_iota(jnp.int32, (rows, keys), 1)
            limit = jnp.minimum(2 * pair + side + 1, WINDOW_BLOCKS + 1) * (2 * rows)
            visible = (col < limit) & ((col <= row + half * rows) | (col >= 2 * rows))
            scores = jnp.where(visible, scores, -jnp.inf)
            top = jnp.max(scores, axis=1, keepdims=True)
            weights = jnp.exp2((scores - top) * factor).astype(jnp.bfloat16)
            extended = jnp.concatenate([value, jnp.ones_like(value)], axis=1)
            mixed = jnp.dot(weights, extended, preferred_element_type=jnp.float32)
            o_here[side, :, cols] = (mixed[:, :HEAD_SIZE] / mixed[:, HEAD_SIZE:]).astype(jnp.bfloat16)
            return 0

        lax.fori_loop(0, 2 * groups, body, 0)

    outs = []

    def give(chunk):
        here = pl.ds(chunk * wide, wide)
        there = pl.ds(pl.multiple_of(core * q_cols + chunk * wide, wide), wide)
        copy = pltpu.make_async_copy(o_here.at[core, :, here], out_ref.at[:, there], o_sem.at[0, chunk])
        copy.start()
        outs.append(copy)
        send(
            o_here.at[1 - core, :, here],
            out_ref.at[:, there],
            o_sem.at[1, chunk],
            o_sem.at[2, chunk],
            mate,
            always,
        )

    for chunk in range(chunks):
        origin(chunk)
        if chunk == 0:
            send(q_part(q_ref, 1 - core), q_here.at[core], q_sem.at[1], q_sem.at[2], mate, always)
    for chunk in range(chunks):
        relay(chunk)
        if chunk == 1:
            q_own.wait()
            pltpu.make_async_copy(q_here.at[1 - core], q_here.at[1 - core], q_sem.at[2]).wait()
        if chunk > 0:
            gather(chunk - 1)
            attend(chunk - 1)
            give(chunk - 1)
    gather(chunks - 1)
    attend(chunks - 1)
    give(chunks - 1)

    for copy, exists in pending:

        @pl.when(exists)
        def _():
            copy.wait_send()

    for chunk in range(chunks):
        outs[chunk].wait()
        there = pl.ds(pl.multiple_of((1 - core) * q_cols + chunk * wide, wide), wide)
        ref = out_ref.at[:, there]
        pltpu.make_async_copy(ref, ref, o_sem.at[2, chunk]).wait()


def on_device_pairs(blocks, queries, keys, values):
    rows = queries.shape[0]
    kv_heads = keys.shape[1] // HEAD_SIZE
    groups = queries.shape[1] // keys.shape[1]
    chunks = kv_heads // 2
    dma = pltpu.SemaphoreType.DMA
    flops = 4 * rows * queries.shape[1] * 8 * rows
    return pl.pallas_call(
        functools.partial(attention_kernel, blocks // 2, groups),
        out_shape=jax.ShapeDtypeStruct(queries.shape, queries.dtype),
        in_specs=[pl.BlockSpec(memory_space=pl.ANY)] * 3,
        out_specs=pl.BlockSpec(memory_space=pl.ANY),
        scratch_shapes=[
            pltpu.VMEM((chunks, 2, 5, 2, rows, HEAD_SIZE), jnp.bfloat16),
            pltpu.VMEM((2, rows, queries.shape[1] // 2), jnp.bfloat16),
            pltpu.VMEM((2, rows, queries.shape[1] // 2), jnp.bfloat16),
            dma((chunks, 2, 2)),
            dma((chunks, 2)),
            dma((chunks, 5, 2)),
            dma((chunks, 10)),
            dma((3,)),
            dma((3, chunks)),
        ],
        compiler_params=pltpu.CompilerParams(
            collective_id=0, has_side_effects=True, vmem_limit_bytes=40 * 2**20
        ),
        cost_estimate=pl.CostEstimate(flops=flops, bytes_accessed=6 * queries.size, transcendentals=flops // 512),
    )(queries, keys, values)


def solution(mesh):
    placed = (P(("ctx", "uly"), None), P(("ctx", "uly"), None), P(("ctx", "uly"), None))
    blocks, halves = mesh.shape["ctx"], mesh.shape["uly"]
    body = on_device
    if halves == 2 and blocks % 4 == 0:
        body = functools.partial(on_device_pairs, blocks)
    return jax.shard_map(
        body, mesh=mesh, in_specs=placed, out_specs=P(("ctx", "uly"), None), check_vma=False
    )
```

```python
import functools

import jax
import jax.numpy as jnp
from jax import lax
from jax.experimental import pallas as pl
from jax.experimental.pallas import tpu as pltpu
from jax.sharding import PartitionSpec as P

HEAD_SIZE = 128
WINDOW_BLOCKS = 3


def passed_along(block, axis, distance):
    devices = range(lax.axis_size(axis))
    route = [(i - distance, i) for i in devices if i - distance in devices]
    return lax.ppermute(block, axis, route)


def on_device(queries, keys, values):
    scale_factor = HEAD_SIZE ** (-0.5)
    cycle_pos = lax.axis_index("ctx")
    query_here, key_here, value_here = (
        lax.all_to_all(queries, "uly", split_axis=1, concat_axis=0, tiled=True),
        lax.all_to_all(keys, "uly", split_axis=1, concat_axis=0, tiled=True),
        lax.all_to_all(values, "uly", split_axis=1, concat_axis=0, tiled=True),
    )
    block_len = query_here.shape[0]
    q_heads = query_here.shape[1] // HEAD_SIZE
    kv_heads = key_here.shape[1] // HEAD_SIZE
    group_size = q_heads // kv_heads
    row_block = min(block_len, 512)
    pieces = block_len // row_block
    item_count = q_heads * pieces
    query_items = (
        query_here.reshape(block_len, q_heads, HEAD_SIZE)
        .transpose(1, 0, 2)
        .reshape(item_count, row_block, HEAD_SIZE)
    )
    key_blocks = key_here.reshape(block_len, kv_heads, HEAD_SIZE).transpose(1, 0, 2)
    value_blocks = value_here.reshape(block_len, kv_heads, HEAD_SIZE).transpose(1, 0, 2)
    carry_state = (
        jnp.full((item_count, row_block), -1e30, jnp.float32),
        jnp.zeros((item_count, row_block), jnp.float32),
        jnp.zeros((item_count, row_block, HEAD_SIZE), jnp.float32),
    )

    def absorb(carry_state, key_set, value_set, step_back):

        def per_item(inputs):
            item_index, running_max, running_sum, weighted, query_rows = inputs
            key_value_index = item_index // (pieces * group_size)
            key_rows = lax.dynamic_index_in_dim(key_set, key_value_index, 0, keepdims=False)
            value_rows = lax.dynamic_index_in_dim(value_set, key_value_index, 0, keepdims=False)
            scores = (
                jnp.einsum("qd,td->qt", query_rows, key_rows, preferred_element_type=jnp.float32)
                * scale_factor
            )
            if step_back == 0:
                query_pos = item_index % pieces * row_block + jnp.arange(row_block, dtype=jnp.int32)
                key_pos = jnp.arange(block_len, dtype=jnp.int32)
                visible = key_pos[None, :] <= query_pos[:, None]
            else:
                visible = jnp.broadcast_to(cycle_pos >= step_back, scores.shape)
            scores = jnp.where(visible, scores, jnp.float32(-1e30))
            new_max = jnp.maximum(running_max, jnp.max(scores, axis=-1))
            weights = jnp.where(visible, jnp.exp(scores - new_max[:, None]), jnp.float32(0.0))
            factor = jnp.exp(running_max - new_max)
            new_sum = running_sum * factor + jnp.sum(weights, axis=-1)
            product = jnp.einsum(
                "qt,td->qd",
                weights.astype(jnp.bfloat16),
                value_rows,
                preferred_element_type=jnp.float32,
            )
            return (new_max, new_sum, weighted * factor[:, None] + product)

        return lax.map(
            per_item,
            (
                jnp.arange(item_count, dtype=jnp.int32),
                carry_state[0],
                carry_state[1],
                carry_state[2],
                query_items,
            ),
        )

    carry_state = absorb(carry_state, key_blocks, value_blocks, 0)
    current = (key_blocks, value_blocks)
    for step_back in range(1, WINDOW_BLOCKS + 1):
        current = passed_along((current[0], current[1]), "ctx", 1)
        carry_state = absorb(carry_state, current[0], current[1], step_back)
    output_rows = (carry_state[2] / carry_state[1][..., None]).astype(jnp.bfloat16)
    output_rows = (
        output_rows.reshape(q_heads, block_len, HEAD_SIZE)
        .transpose(1, 0, 2)
        .reshape(block_len, q_heads * HEAD_SIZE)
    )
    return lax.all_to_all(output_rows, "uly", split_axis=0, concat_axis=1, tiled=True)


MESH = pl.DeviceIdType.MESH
LOG2_E = 1.4426950408889634


def attention_kernel(
    pairs,
    groups,
    q_ref,
    k_ref,
    v_ref,
    out_ref,
    kv,
    q_here,
    o_here,
    bias,
    counted,
    own_sem,
    pair_send,
    slot_sem,
    send_sem,
    q_sem,
    o_sem,
):
    ctx = lax.axis_index("ctx")
    half = lax.axis_index("uly")
    other = 1 - half
    pair, core = ctx // 2, lax.rem(ctx, 2)
    odd = lax.rem(pair, 2)
    chunks = kv.shape[0]
    rows = q_ref.shape[0]
    q_cols = q_ref.shape[1] // 2
    wide = q_cols // chunks

    mate = (2 * pair + 1 - core, half)
    across = (ctx, other)
    ahead1, ahead2 = (ctx + 2, half), (ctx + 4, half)
    behind1, behind2 = (ctx - 2, half), (ctx - 4, half)
    has_a1, has_a2 = pair + 1 < pairs, pair + 2 < pairs
    has_b1, has_b2 = pair >= 1, pair >= 2
    even = odd == 0
    always = pair >= 0

    barrier = pltpu.get_barrier_semaphore()
    count = jnp.int32(0)
    for device, exists in (
        (mate, always),
        (across, always),
        (ahead1, has_a1),
        (ahead2, has_a2),
        (behind1, has_b1),
        (behind2, has_b2),
    ):
        count += exists.astype(jnp.int32)

        @pl.when(exists)
        def _():
            pl.semaphore_signal(barrier, inc=1, device_id=device, device_id_type=MESH)

    def column(ref, head):
        return ref.at[:, pl.ds(pl.multiple_of(head * HEAD_SIZE, HEAD_SIZE), HEAD_SIZE)]

    def q_part(ref, index):
        return ref.at[:, pl.ds(pl.multiple_of(index * q_cols, q_cols), q_cols)]

    own = []
    for chunk in range(chunks):
        for which, ref in enumerate((k_ref, v_ref)):
            copy = pltpu.make_async_copy(
                column(ref, core * chunks + chunk),
                kv.at[chunk, which, 1 - core, half],
                own_sem.at[chunk, 1 - core, which],
            )
            copy.start()
    q_own = pltpu.make_async_copy(q_part(q_ref, core), q_here.at[core], q_sem.at[0])
    q_own.start()

    @pl.when(pair < 2)
    def _():
        for d in (2, 3, 4):

            @pl.when(2 * pair + 1 - d < 0)
            def _():
                kv[:, 1, d] = jnp.zeros_like(kv[:, 1, d])

    pl.semaphore_wait(barrier, count)

    pending = []

    def send(src, dst, sent, landed, device, exists):
        copy = pltpu.make_async_remote_copy(
            src_ref=src, dst_ref=dst, send_sem=sent, recv_sem=landed, device_id=device, device_id_type=MESH
        )

        @pl.when(exists)
        def _():
            copy.start()

        pending.append((copy, exists))

    for chunk in range(chunks):
        for which, ref in enumerate((k_ref, v_ref)):
            send(
                column(ref, (1 - core) * chunks + chunk),
                kv.at[chunk, which, 1 - core, half],
                pair_send.at[chunk, which],
                own_sem.at[chunk, 1 - core, which],
                mate,
                always,
            )
    def await_own(chunk, d):
        for which in range(2):
            ref = kv.at[chunk, which, d, half]
            pltpu.make_async_copy(ref, ref, own_sem.at[chunk, d, which]).wait()

    def await_slot(chunk, d, side, exists=None):
        ref = kv.at[chunk, :, d, side]
        copy = pltpu.make_async_copy(ref, ref, slot_sem.at[chunk, d, side])
        if exists is None:
            copy.wait()
        else:

            @pl.when(exists)
            def _():
                copy.wait()

    def pass_on(chunk, src_d, dst_d, side, route, device, exists):
        send(
            kv.at[chunk, :, src_d, side],
            kv.at[chunk, :, dst_d, side],
            send_sem.at[chunk, route],
            slot_sem.at[chunk, dst_d, side],
            device,
            exists,
        )

    def origin(chunk):
        await_own(chunk, 0)
        pass_on(chunk, 0, 0, half, 0, across, always)
        pass_on(chunk, 0, 4, half, 1, ahead2, has_a2)
        pass_on(chunk, 0, 2, half, 2, ahead1, has_a1 & even)
        await_own(chunk, 1)
        pass_on(chunk, 1, 3, half, 3, ahead1, has_a1)
        pass_on(chunk, 1, 1, half, 4, across, always)

    def relay(chunk):
        await_slot(chunk, 0, other)
        pass_on(chunk, 0, 4, other, 5, ahead2, has_a2)
        pass_on(chunk, 0, 2, other, 6, ahead1, has_a1 & even)
        await_slot(chunk, 3, half, has_b1)
        pass_on(chunk, 3, 3, half, 7, across, has_b1)
        from_far = has_b2 & (odd == 1)
        await_slot(chunk, 4, half, from_far)
        pass_on(chunk, 4, 2, half, 8, behind1, from_far)
        await_slot(chunk, 4, other, from_far)
        pass_on(chunk, 4, 2, other, 9, behind1, from_far)

    def gather(chunk):
        await_slot(chunk, 1, other)
        await_slot(chunk, 4, half, has_b2 & even)
        await_slot(chunk, 4, other, has_b2 & even)
        await_slot(chunk, 3, other, has_b1)
        await_slot(chunk, 2, half, has_b1)
        await_slot(chunk, 2, other, has_b1)

    factor = HEAD_SIZE ** (-0.5) * LOG2_E
    keys = 8 * rows
    row = lax.broadcasted_iota(jnp.int32, bias.shape, 0)
    col = lax.broadcasted_iota(jnp.int32, bias.shape, 1)
    bias[...] = jnp.where(col <= row + half * rows, 0.0, -1e30)
    counted[...] = jnp.ones_like(counted)

    @pl.when(pair < 2)
    def _():
        for d in (2, 3, 4):

            @pl.when(2 * pair + 1 - d < 0)
            def _():
                counted[d] = jnp.zeros_like(counted[d])

    def attend(chunk):
        @pl.when(pair < 2)
        def _():
            seen = jnp.broadcast_to(kv[chunk, 0, 1, 0][:1], (rows, HEAD_SIZE))
            for d in (2, 3, 4):

                @pl.when(2 * pair + 1 - d < 0)
                def _():
                    kv[chunk, 0, d, 0] = seen
                    kv[chunk, 0, d, 1] = seen

        for side in range(2):
            first = 1 - side
            heads = [pl.ds(chunk * wide + head * HEAD_SIZE, HEAD_SIZE) for head in range(groups)]
            query = jnp.concatenate([q_here[side, :, cols] for cols in heads], axis=0)
            key = kv[chunk, 0, first : first + 4].reshape(keys, HEAD_SIZE)
            value = kv[chunk, 1, first : first + 4].reshape(keys, HEAD_SIZE)
            ones = counted[first : first + 4].reshape(keys, HEAD_SIZE)
            scores = lax.dot_general(
                query, key, (((1,), (1,)), ((), ())), preferred_element_type=jnp.float32
            )
            parts = []
            for head in range(groups):
                part = scores[head * rows : (head + 1) * rows]
                part = jnp.concatenate([part[:, : 2 * rows] + bias[...], part[:, 2 * rows :]], axis=1)
                top = jnp.max(part, axis=1, keepdims=True)
                parts.append(jnp.exp2((part - top) * factor).astype(jnp.bfloat16))
            mixed = jnp.dot(
                jnp.concatenate(parts, axis=0),
                jnp.concatenate([value, ones], axis=1),
                preferred_element_type=jnp.float32,
            )
            result = (mixed[:, :HEAD_SIZE] / mixed[:, HEAD_SIZE:]).astype(jnp.bfloat16)
            for head, cols in enumerate(heads):
                o_here[side, :, cols] = result[head * rows : (head + 1) * rows]

    outs = []

    def give(chunk):
        here = pl.ds(chunk * wide, wide)
        there = pl.ds(pl.multiple_of(core * q_cols + chunk * wide, wide), wide)
        copy = pltpu.make_async_copy(o_here.at[core, :, here], out_ref.at[:, there], o_sem.at[0, chunk])
        copy.start()
        outs.append(copy)
        send(
            o_here.at[1 - core, :, here],
            out_ref.at[:, there],
            o_sem.at[1, chunk],
            o_sem.at[2, chunk],
            mate,
            always,
        )

    for chunk in range(chunks):
        origin(chunk)
        if chunk == 0:
            send(q_part(q_ref, 1 - core), q_here.at[core], q_sem.at[1], q_sem.at[2], mate, always)
    for chunk in range(chunks):
        relay(chunk)
        if chunk == 1:
            q_own.wait()
            pltpu.make_async_copy(q_here.at[1 - core], q_here.at[1 - core], q_sem.at[2]).wait()
        if chunk > 0:
            gather(chunk - 1)
            attend(chunk - 1)
            give(chunk - 1)
    gather(chunks - 1)
    attend(chunks - 1)
    give(chunks - 1)

    for copy, exists in pending:

        @pl.when(exists)
        def _():
            copy.wait_send()

    for chunk in range(chunks):
        outs[chunk].wait()
        there = pl.ds(pl.multiple_of((1 - core) * q_cols + chunk * wide, wide), wide)
        ref = out_ref.at[:, there]
        pltpu.make_async_copy(ref, ref, o_sem.at[2, chunk]).wait()


def on_device_pairs(blocks, queries, keys, values):
    rows = queries.shape[0]
    kv_heads = keys.shape[1] // HEAD_SIZE
    groups = queries.shape[1] // keys.shape[1]
    chunks = kv_heads // 2
    dma = pltpu.SemaphoreType.DMA
    flops = 4 * rows * queries.shape[1] * 8 * rows
    return pl.pallas_call(
        functools.partial(attention_kernel, blocks // 2, groups),
        out_shape=jax.ShapeDtypeStruct(queries.shape, queries.dtype),
        in_specs=[pl.BlockSpec(memory_space=pltpu.HBM)] * 3,
        out_specs=pl.BlockSpec(memory_space=pltpu.HBM),
        scratch_shapes=[
            pltpu.VMEM((chunks, 2, 5, 2, rows, HEAD_SIZE), jnp.bfloat16),
            pltpu.VMEM((2, rows, queries.shape[1] // 2), jnp.bfloat16),
            pltpu.VMEM((2, rows, queries.shape[1] // 2), jnp.bfloat16),
            pltpu.VMEM((rows, 2 * rows), jnp.float32),
            pltpu.VMEM((5, 2, rows, HEAD_SIZE), jnp.bfloat16),
            dma((chunks, 2, 2)),
            dma((chunks, 2)),
            dma((chunks, 5, 2)),
            dma((chunks, 10)),
            dma((3,)),
            dma((3, chunks)),
        ],
        compiler_params=pltpu.CompilerParams(
            collective_id=0, has_side_effects=True, vmem_limit_bytes=60 * 2**20
        ),
        cost_estimate=pl.CostEstimate(flops=flops, bytes_accessed=6 * queries.size, transcendentals=flops // 512),
    )(queries, keys, values)


def solution(mesh):
    placed = (P(("ctx", "uly"), None), P(("ctx", "uly"), None), P(("ctx", "uly"), None))
    blocks, halves = mesh.shape["ctx"], mesh.shape["uly"]
    body = on_device
    if halves == 2 and blocks % 4 == 0:
        body = functools.partial(on_device_pairs, blocks)
    return jax.shard_map(
        body, mesh=mesh, in_specs=placed, out_specs=P(("ctx", "uly"), None), check_vma=False
    )
```

```python
import functools

import jax
import jax.numpy as jnp
from jax import lax
from jax.experimental import pallas as pl
from jax.experimental.pallas import tpu as pltpu
from jax.sharding import PartitionSpec as P

HEAD_SIZE = 128
WINDOW_BLOCKS = 3


def passed_along(block, axis, distance):
    devices = range(lax.axis_size(axis))
    route = [(i - distance, i) for i in devices if i - distance in devices]
    return lax.ppermute(block, axis, route)


def on_device(queries, keys, values):
    scale_factor = HEAD_SIZE ** (-0.5)
    cycle_pos = lax.axis_index("ctx")
    query_here, key_here, value_here = (
        lax.all_to_all(queries, "uly", split_axis=1, concat_axis=0, tiled=True),
        lax.all_to_all(keys, "uly", split_axis=1, concat_axis=0, tiled=True),
        lax.all_to_all(values, "uly", split_axis=1, concat_axis=0, tiled=True),
    )
    block_len = query_here.shape[0]
    q_heads = query_here.shape[1] // HEAD_SIZE
    kv_heads = key_here.shape[1] // HEAD_SIZE
    group_size = q_heads // kv_heads
    row_block = min(block_len, 512)
    pieces = block_len // row_block
    item_count = q_heads * pieces
    query_items = (
        query_here.reshape(block_len, q_heads, HEAD_SIZE)
        .transpose(1, 0, 2)
        .reshape(item_count, row_block, HEAD_SIZE)
    )
    key_blocks = key_here.reshape(block_len, kv_heads, HEAD_SIZE).transpose(1, 0, 2)
    value_blocks = value_here.reshape(block_len, kv_heads, HEAD_SIZE).transpose(1, 0, 2)
    carry_state = (
        jnp.full((item_count, row_block), -1e30, jnp.float32),
        jnp.zeros((item_count, row_block), jnp.float32),
        jnp.zeros((item_count, row_block, HEAD_SIZE), jnp.float32),
    )

    def absorb(carry_state, key_set, value_set, step_back):

        def per_item(inputs):
            item_index, running_max, running_sum, weighted, query_rows = inputs
            key_value_index = item_index // (pieces * group_size)
            key_rows = lax.dynamic_index_in_dim(key_set, key_value_index, 0, keepdims=False)
            value_rows = lax.dynamic_index_in_dim(value_set, key_value_index, 0, keepdims=False)
            scores = (
                jnp.einsum("qd,td->qt", query_rows, key_rows, preferred_element_type=jnp.float32)
                * scale_factor
            )
            if step_back == 0:
                query_pos = item_index % pieces * row_block + jnp.arange(row_block, dtype=jnp.int32)
                key_pos = jnp.arange(block_len, dtype=jnp.int32)
                visible = key_pos[None, :] <= query_pos[:, None]
            else:
                visible = jnp.broadcast_to(cycle_pos >= step_back, scores.shape)
            scores = jnp.where(visible, scores, jnp.float32(-1e30))
            new_max = jnp.maximum(running_max, jnp.max(scores, axis=-1))
            weights = jnp.where(visible, jnp.exp(scores - new_max[:, None]), jnp.float32(0.0))
            factor = jnp.exp(running_max - new_max)
            new_sum = running_sum * factor + jnp.sum(weights, axis=-1)
            product = jnp.einsum(
                "qt,td->qd",
                weights.astype(jnp.bfloat16),
                value_rows,
                preferred_element_type=jnp.float32,
            )
            return (new_max, new_sum, weighted * factor[:, None] + product)

        return lax.map(
            per_item,
            (
                jnp.arange(item_count, dtype=jnp.int32),
                carry_state[0],
                carry_state[1],
                carry_state[2],
                query_items,
            ),
        )

    carry_state = absorb(carry_state, key_blocks, value_blocks, 0)
    current = (key_blocks, value_blocks)
    for step_back in range(1, WINDOW_BLOCKS + 1):
        current = passed_along((current[0], current[1]), "ctx", 1)
        carry_state = absorb(carry_state, current[0], current[1], step_back)
    output_rows = (carry_state[2] / carry_state[1][..., None]).astype(jnp.bfloat16)
    output_rows = (
        output_rows.reshape(q_heads, block_len, HEAD_SIZE)
        .transpose(1, 0, 2)
        .reshape(block_len, q_heads * HEAD_SIZE)
    )
    return lax.all_to_all(output_rows, "uly", split_axis=0, concat_axis=1, tiled=True)


MESH = pl.DeviceIdType.MESH
LOG2_E = 1.4426950408889634


def attention_kernel(
    pairs,
    groups,
    q_ref,
    k_ref,
    v_ref,
    out_ref,
    kv,
    q_here,
    o_here,
    bias,
    counted,
    own_sem,
    pair_send,
    slot_sem,
    send_sem,
    q_sem,
    o_sem,
):
    ctx = lax.axis_index("ctx")
    half = lax.axis_index("uly")
    other = 1 - half
    pair, core = ctx // 2, lax.rem(ctx, 2)
    odd = lax.rem(pair, 2)
    chunks = kv.shape[0]
    rows = q_ref.shape[0]
    q_cols = q_ref.shape[1] // 2
    wide = q_cols // chunks

    mate = (2 * pair + 1 - core, half)
    across = (ctx, other)
    ahead1, ahead2 = (ctx + 2, half), (ctx + 4, half)
    behind1, behind2 = (ctx - 2, half), (ctx - 4, half)
    has_a1, has_a2 = pair + 1 < pairs, pair + 2 < pairs
    has_b1, has_b2 = pair >= 1, pair >= 2
    even = odd == 0
    always = pair >= 0

    barrier = pltpu.get_barrier_semaphore()
    count = jnp.int32(0)
    for device, exists in (
        (mate, always),
        (across, always),
        (ahead1, has_a1),
        (ahead2, has_a2),
        (behind1, has_b1),
        (behind2, has_b2),
    ):
        count += exists.astype(jnp.int32)

        @pl.when(exists)
        def _():
            pl.semaphore_signal(barrier, inc=1, device_id=device, device_id_type=MESH)

    def column(ref, head):
        return ref.at[:, pl.ds(pl.multiple_of(head * HEAD_SIZE, HEAD_SIZE), HEAD_SIZE)]

    def q_part(ref, index):
        return ref.at[:, pl.ds(pl.multiple_of(index * q_cols, q_cols), q_cols)]

    own = []
    for chunk in range(chunks):
        for which, ref in enumerate((k_ref, v_ref)):
            copy = pltpu.make_async_copy(
                column(ref, core * chunks + chunk),
                kv.at[chunk, which, 1 - core, half],
                own_sem.at[chunk, 1 - core, which],
            )
            copy.start()
    q_own = pltpu.make_async_copy(q_part(q_ref, core), q_here.at[core], q_sem.at[0])
    q_own.start()

    @pl.when(pair < 2)
    def _():
        for d in (2, 3, 4):

            @pl.when(2 * pair + 1 - d < 0)
            def _():
                kv[:, 1, d] = jnp.zeros_like(kv[:, 1, d])

    pl.semaphore_wait(barrier, count)

    pending = []

    def send(src, dst, sent, landed, device, exists):
        copy = pltpu.make_async_remote_copy(
            src_ref=src, dst_ref=dst, send_sem=sent, recv_sem=landed, device_id=device, device_id_type=MESH
        )

        @pl.when(exists)
        def _():
            copy.start()

        pending.append((copy, exists))

    for chunk in range(chunks):
        for which, ref in enumerate((k_ref, v_ref)):
            send(
                column(ref, (1 - core) * chunks + chunk),
                kv.at[chunk, which, 1 - core, half],
                pair_send.at[chunk, which],
                own_sem.at[chunk, 1 - core, which],
                mate,
                always,
            )
    def await_own(chunk, d):
        for which in range(2):
            ref = kv.at[chunk, which, d, half]
            pltpu.make_async_copy(ref, ref, own_sem.at[chunk, d, which]).wait()

    def await_slot(chunk, d, side, exists=None):
        ref = kv.at[chunk, :, d, side]
        copy = pltpu.make_async_copy(ref, ref, slot_sem.at[chunk, d, side])
        if exists is None:
            copy.wait()
        else:

            @pl.when(exists)
            def _():
                copy.wait()

    def pass_on(chunk, src_d, dst_d, side, route, device, exists):
        send(
            kv.at[chunk, :, src_d, side],
            kv.at[chunk, :, dst_d, side],
            send_sem.at[chunk, route],
            slot_sem.at[chunk, dst_d, side],
            device,
            exists,
        )

    from_far = has_b2 & (odd == 1)

    def origin(chunk):
        await_own(chunk, 0)
        pass_on(chunk, 0, 0, half, 0, across, always)
        pass_on(chunk, 0, 4, half, 1, ahead2, has_a2)
        await_own(chunk, 1)
        pass_on(chunk, 1, 3, half, 3, ahead1, has_a1)
        pass_on(chunk, 0, 2, half, 2, ahead1, has_a1 & even)

    def cross_last(chunk):
        pass_on(chunk, 1, 1, half, 4, across, always)

    def relay_first(chunk):
        await_slot(chunk, 0, other)
        pass_on(chunk, 0, 4, other, 5, ahead2, has_a2)
        pass_on(chunk, 0, 2, other, 6, ahead1, has_a1 & even)

    def relay_cross(chunk):
        await_slot(chunk, 3, half, has_b1)
        pass_on(chunk, 3, 3, half, 7, across, has_b1)

    def relay_own(chunk):
        await_slot(chunk, 4, half, from_far)
        pass_on(chunk, 4, 2, half, 8, behind1, from_far)

    def relay_other(chunk):
        await_slot(chunk, 4, other, from_far)
        pass_on(chunk, 4, 2, other, 9, behind1, from_far)

    def gather(chunk):
        await_slot(chunk, 1, other)
        await_slot(chunk, 4, half, has_b2 & even)
        await_slot(chunk, 4, other, has_b2 & even)
        await_slot(chunk, 3, other, has_b1)
        await_slot(chunk, 2, half, has_b1)
        await_slot(chunk, 2, other, has_b1)

    factor = HEAD_SIZE ** (-0.5) * LOG2_E
    keys = 8 * rows
    row = lax.broadcasted_iota(jnp.int32, bias.shape, 0)
    col = lax.broadcasted_iota(jnp.int32, bias.shape, 1)
    bias[...] = jnp.where(col <= row + half * rows, 0.0, -1e30)
    counted[...] = jnp.ones_like(counted)

    @pl.when(pair < 2)
    def _():
        for d in (2, 3, 4):

            @pl.when(2 * pair + 1 - d < 0)
            def _():
                counted[d] = jnp.zeros_like(counted[d])

    def attend(chunk):
        @pl.when(pair < 2)
        def _():
            seen = jnp.broadcast_to(kv[chunk, 0, 1, 0][:1], (rows, HEAD_SIZE))
            for d in (2, 3, 4):

                @pl.when(2 * pair + 1 - d < 0)
                def _():
                    kv[chunk, 0, d, 0] = seen
                    kv[chunk, 0, d, 1] = seen

        for side in range(2):
            first = 1 - side
            heads = [pl.ds(chunk * wide + head * HEAD_SIZE, HEAD_SIZE) for head in range(groups)]
            query = jnp.concatenate([q_here[side, :, cols] for cols in heads], axis=0)
            key = kv[chunk, 0, first : first + 4].reshape(keys, HEAD_SIZE)
            value = kv[chunk, 1, first : first + 4].reshape(keys, HEAD_SIZE)
            ones = counted[first : first + 4].reshape(keys, HEAD_SIZE)
            scores = lax.dot_general(
                query, key, (((1,), (1,)), ((), ())), preferred_element_type=jnp.float32
            )
            parts = []
            for head in range(groups):
                part = scores[head * rows : (head + 1) * rows]
                part = jnp.concatenate([part[:, : 2 * rows] + bias[...], part[:, 2 * rows :]], axis=1)
                top = jnp.max(part, axis=1, keepdims=True)
                parts.append(jnp.exp2((part - top) * factor).astype(jnp.bfloat16))
            mixed = jnp.dot(
                jnp.concatenate(parts, axis=0),
                jnp.concatenate([value, ones], axis=1),
                preferred_element_type=jnp.float32,
            )
            result = (mixed[:, :HEAD_SIZE] / mixed[:, HEAD_SIZE:]).astype(jnp.bfloat16)
            for head, cols in enumerate(heads):
                o_here[side, :, cols] = result[head * rows : (head + 1) * rows]

    outs = []

    def give(chunk):
        here = pl.ds(chunk * wide, wide)
        there = pl.ds(pl.multiple_of(core * q_cols + chunk * wide, wide), wide)
        copy = pltpu.make_async_copy(o_here.at[core, :, here], out_ref.at[:, there], o_sem.at[0, chunk])
        copy.start()
        outs.append(copy)
        send(
            o_here.at[1 - core, :, here],
            out_ref.at[:, there],
            o_sem.at[1, chunk],
            o_sem.at[2, chunk],
            mate,
            always,
        )

    def ask(_):
        send(q_part(q_ref, 1 - core), q_here.at[core], q_sem.at[1], q_sem.at[2], mate, always)

    def await_queries(_):
        q_own.wait()
        pltpu.make_async_copy(q_here.at[1 - core], q_here.at[1 - core], q_sem.at[2]).wait()

    def finish(chunk):
        gather(chunk)
        attend(chunk)
        give(chunk)

    for chunk in range(chunks + 2):
        if chunk < chunks:
            origin(chunk)
            if chunk == 0:
                ask(chunk)
        if 0 < chunk <= chunks:
            relay_first(chunk - 1)
            relay_cross(chunk - 1)
            relay_own(chunk - 1)
            cross_last(chunk - 1)
        if 1 < chunk:
            relay_other(chunk - 2)
            if chunk == 2:
                await_queries(chunk)
            if chunk > 2:
                finish(chunk - 3)
    finish(chunks - 1)
    for copy, exists in pending:

        @pl.when(exists)
        def _():
            copy.wait_send()

    for chunk in range(chunks):
        outs[chunk].wait()
        there = pl.ds(pl.multiple_of((1 - core) * q_cols + chunk * wide, wide), wide)
        ref = out_ref.at[:, there]
        pltpu.make_async_copy(ref, ref, o_sem.at[2, chunk]).wait()


def on_device_pairs(blocks, queries, keys, values):
    rows = queries.shape[0]
    kv_heads = keys.shape[1] // HEAD_SIZE
    groups = queries.shape[1] // keys.shape[1]
    chunks = kv_heads // 2
    dma = pltpu.SemaphoreType.DMA
    flops = 4 * rows * queries.shape[1] * 8 * rows
    queries, keys, values = (pltpu.with_memory_space_constraint(a, pltpu.HBM) for a in (queries, keys, values))
    return pl.pallas_call(
        functools.partial(attention_kernel, blocks // 2, groups),
        out_shape=jax.ShapeDtypeStruct(queries.shape, queries.dtype),
        in_specs=[pl.BlockSpec(memory_space=pltpu.HBM)] * 3,
        out_specs=pl.BlockSpec(memory_space=pl.ANY),
        scratch_shapes=[
            pltpu.VMEM((chunks, 2, 5, 2, rows, HEAD_SIZE), jnp.bfloat16),
            pltpu.VMEM((2, rows, queries.shape[1] // 2), jnp.bfloat16),
            pltpu.VMEM((2, rows, queries.shape[1] // 2), jnp.bfloat16),
            pltpu.VMEM((rows, 2 * rows), jnp.float32),
            pltpu.VMEM((5, 2, rows, HEAD_SIZE), jnp.bfloat16),
            dma((chunks, 2, 2)),
            dma((chunks, 2)),
            dma((chunks, 5, 2)),
            dma((chunks, 10)),
            dma((3,)),
            dma((3, chunks)),
        ],
        compiler_params=pltpu.CompilerParams(
            collective_id=0, has_side_effects=True, vmem_limit_bytes=32 * 2**20
        ),
        cost_estimate=pl.CostEstimate(flops=flops, bytes_accessed=6 * queries.size, transcendentals=flops // 512),
    )(queries, keys, values)


def solution(mesh):
    placed = (P(("ctx", "uly"), None), P(("ctx", "uly"), None), P(("ctx", "uly"), None))
    blocks, halves = mesh.shape["ctx"], mesh.shape["uly"]
    body = on_device
    if halves == 2 and blocks % 4 == 0:
        body = functools.partial(on_device_pairs, blocks)
    return jax.shard_map(
        body, mesh=mesh, in_specs=placed, out_specs=P(("ctx", "uly"), None), check_vma=False
    )
```

```python
import functools

import jax
import jax.numpy as jnp
from jax import lax
from jax.experimental import pallas as pl
from jax.experimental.pallas import tpu as pltpu
from jax.sharding import PartitionSpec as P

HEAD_SIZE = 128
WINDOW_BLOCKS = 3


def passed_along(block, axis, distance):
    devices = range(lax.axis_size(axis))
    route = [(i - distance, i) for i in devices if i - distance in devices]
    return lax.ppermute(block, axis, route)


def on_device(queries, keys, values):
    scale_factor = HEAD_SIZE ** (-0.5)
    cycle_pos = lax.axis_index("ctx")
    query_here, key_here, value_here = (
        lax.all_to_all(queries, "uly", split_axis=1, concat_axis=0, tiled=True),
        lax.all_to_all(keys, "uly", split_axis=1, concat_axis=0, tiled=True),
        lax.all_to_all(values, "uly", split_axis=1, concat_axis=0, tiled=True),
    )
    block_len = query_here.shape[0]
    q_heads = query_here.shape[1] // HEAD_SIZE
    kv_heads = key_here.shape[1] // HEAD_SIZE
    group_size = q_heads // kv_heads
    row_block = min(block_len, 512)
    pieces = block_len // row_block
    item_count = q_heads * pieces
    query_items = (
        query_here.reshape(block_len, q_heads, HEAD_SIZE)
        .transpose(1, 0, 2)
        .reshape(item_count, row_block, HEAD_SIZE)
    )
    key_blocks = key_here.reshape(block_len, kv_heads, HEAD_SIZE).transpose(1, 0, 2)
    value_blocks = value_here.reshape(block_len, kv_heads, HEAD_SIZE).transpose(1, 0, 2)
    carry_state = (
        jnp.full((item_count, row_block), -1e30, jnp.float32),
        jnp.zeros((item_count, row_block), jnp.float32),
        jnp.zeros((item_count, row_block, HEAD_SIZE), jnp.float32),
    )

    def absorb(carry_state, key_set, value_set, step_back):

        def per_item(inputs):
            item_index, running_max, running_sum, weighted, query_rows = inputs
            key_value_index = item_index // (pieces * group_size)
            key_rows = lax.dynamic_index_in_dim(key_set, key_value_index, 0, keepdims=False)
            value_rows = lax.dynamic_index_in_dim(value_set, key_value_index, 0, keepdims=False)
            scores = (
                jnp.einsum("qd,td->qt", query_rows, key_rows, preferred_element_type=jnp.float32)
                * scale_factor
            )
            if step_back == 0:
                query_pos = item_index % pieces * row_block + jnp.arange(row_block, dtype=jnp.int32)
                key_pos = jnp.arange(block_len, dtype=jnp.int32)
                visible = key_pos[None, :] <= query_pos[:, None]
            else:
                visible = jnp.broadcast_to(cycle_pos >= step_back, scores.shape)
            scores = jnp.where(visible, scores, jnp.float32(-1e30))
            new_max = jnp.maximum(running_max, jnp.max(scores, axis=-1))
            weights = jnp.where(visible, jnp.exp(scores - new_max[:, None]), jnp.float32(0.0))
            factor = jnp.exp(running_max - new_max)
            new_sum = running_sum * factor + jnp.sum(weights, axis=-1)
            product = jnp.einsum(
                "qt,td->qd",
                weights.astype(jnp.bfloat16),
                value_rows,
                preferred_element_type=jnp.float32,
            )
            return (new_max, new_sum, weighted * factor[:, None] + product)

        return lax.map(
            per_item,
            (
                jnp.arange(item_count, dtype=jnp.int32),
                carry_state[0],
                carry_state[1],
                carry_state[2],
                query_items,
            ),
        )

    carry_state = absorb(carry_state, key_blocks, value_blocks, 0)
    current = (key_blocks, value_blocks)
    for step_back in range(1, WINDOW_BLOCKS + 1):
        current = passed_along((current[0], current[1]), "ctx", 1)
        carry_state = absorb(carry_state, current[0], current[1], step_back)
    output_rows = (carry_state[2] / carry_state[1][..., None]).astype(jnp.bfloat16)
    output_rows = (
        output_rows.reshape(q_heads, block_len, HEAD_SIZE)
        .transpose(1, 0, 2)
        .reshape(block_len, q_heads * HEAD_SIZE)
    )
    return lax.all_to_all(output_rows, "uly", split_axis=0, concat_axis=1, tiled=True)


MESH = pl.DeviceIdType.MESH
LOG2_E = 1.4426950408889634


def attention_kernel(
    pairs,
    groups,
    q_ref,
    k_ref,
    v_ref,
    out_ref,
    kv,
    q_here,
    o_here,
    bias,
    counted,
    own_sem,
    pair_send,
    slot_sem,
    send_sem,
    q_sem,
    o_sem,
):
    ctx = lax.axis_index("ctx")
    half = lax.axis_index("uly")
    other = 1 - half
    pair, core = ctx // 2, lax.rem(ctx, 2)
    odd = lax.rem(pair, 2)
    chunks = kv.shape[0]
    rows = q_ref.shape[0]
    q_cols = q_ref.shape[1] // 2
    wide = q_cols // chunks

    mate = (2 * pair + 1 - core, half)
    across = (ctx, other)
    ahead1, ahead2 = (ctx + 2, half), (ctx + 4, half)
    behind1, behind2 = (ctx - 2, half), (ctx - 4, half)
    has_a1, has_a2 = pair + 1 < pairs, pair + 2 < pairs
    has_b1, has_b2 = pair >= 1, pair >= 2
    even = odd == 0
    always = pair >= 0

    barrier = pltpu.get_barrier_semaphore()
    count = jnp.int32(0)
    for device, exists in (
        (mate, always),
        (across, always),
        (ahead1, has_a1),
        (ahead2, has_a2),
        (behind1, has_b1),
        (behind2, has_b2),
    ):
        count += exists.astype(jnp.int32)

        @pl.when(exists)
        def _():
            pl.semaphore_signal(barrier, inc=1, device_id=device, device_id_type=MESH)

    def column(ref, head):
        return ref.at[:, pl.ds(pl.multiple_of(head * HEAD_SIZE, HEAD_SIZE), HEAD_SIZE)]

    def q_part(ref, index):
        return ref.at[:, pl.ds(pl.multiple_of(index * q_cols, q_cols), q_cols)]

    own = []
    for chunk in range(chunks):
        for which, ref in enumerate((k_ref, v_ref)):
            copy = pltpu.make_async_copy(
                column(ref, core * chunks + chunk),
                kv.at[chunk, which, 1 - core, half],
                own_sem.at[chunk, 1 - core, which],
            )
            copy.start()
    q_own = pltpu.make_async_copy(q_part(q_ref, core), q_here.at[core], q_sem.at[0])
    q_own.start()

    @pl.when(pair < 2)
    def _():
        for d in (2, 3, 4):

            @pl.when(2 * pair + 1 - d < 0)
            def _():
                kv[:, 1, d] = jnp.zeros_like(kv[:, 1, d])

    pl.semaphore_wait(barrier, count)

    pending = []

    def send(src, dst, sent, landed, device, exists):
        copy = pltpu.make_async_remote_copy(
            src_ref=src, dst_ref=dst, send_sem=sent, recv_sem=landed, device_id=device, device_id_type=MESH
        )

        @pl.when(exists)
        def _():
            copy.start()

        pending.append((copy, exists))

    for chunk in range(chunks):
        for which, ref in enumerate((k_ref, v_ref)):
            send(
                column(ref, (1 - core) * chunks + chunk),
                kv.at[chunk, which, 1 - core, half],
                pair_send.at[chunk, which],
                own_sem.at[chunk, 1 - core, which],
                mate,
                always,
            )
    def await_own(chunk, d):
        for which in range(2):
            ref = kv.at[chunk, which, d, half]
            pltpu.make_async_copy(ref, ref, own_sem.at[chunk, d, which]).wait()

    def await_slot(chunk, d, side, exists=None):
        ref = kv.at[chunk, :, d, side]
        copy = pltpu.make_async_copy(ref, ref, slot_sem.at[chunk, d, side])
        if exists is None:
            copy.wait()
        else:

            @pl.when(exists)
            def _():
                copy.wait()

    def pass_on(chunk, src_d, dst_d, side, route, device, exists):
        send(
            kv.at[chunk, :, src_d, side],
            kv.at[chunk, :, dst_d, side],
            send_sem.at[chunk, route],
            slot_sem.at[chunk, dst_d, side],
            device,
            exists,
        )

    from_far = has_b2 & (odd == 1)

    def origin(chunk):
        await_own(chunk, 0)
        pass_on(chunk, 0, 0, half, 0, across, always)
        pass_on(chunk, 0, 4, half, 1, ahead2, has_a2)
        await_own(chunk, 1)
        pass_on(chunk, 1, 3, half, 3, ahead1, has_a1)
        pass_on(chunk, 0, 2, half, 2, ahead1, has_a1 & even)

    def cross_last(chunk):
        pass_on(chunk, 1, 1, half, 4, across, always)

    def relay_first(chunk):
        await_slot(chunk, 0, other)
        pass_on(chunk, 0, 4, other, 5, ahead2, has_a2)
        pass_on(chunk, 0, 2, other, 6, ahead1, has_a1 & even)

    def relay_cross(chunk):
        await_slot(chunk, 3, half, has_b1)
        pass_on(chunk, 3, 3, half, 7, across, has_b1)

    def relay_own(chunk):
        await_slot(chunk, 4, half, from_far)
        pass_on(chunk, 4, 2, half, 8, behind1, from_far)

    def relay_other(chunk):
        await_slot(chunk, 4, other, from_far)
        pass_on(chunk, 4, 2, other, 9, behind1, from_far)

    def gather(chunk):
        await_slot(chunk, 1, other)
        await_slot(chunk, 4, half, has_b2 & even)
        await_slot(chunk, 4, other, has_b2 & even)
        await_slot(chunk, 3, other, has_b1)
        await_slot(chunk, 2, half, has_b1)
        await_slot(chunk, 2, other, has_b1)

    factor = HEAD_SIZE ** (-0.5) * LOG2_E
    keys = 8 * rows
    row = lax.broadcasted_iota(jnp.int32, bias.shape, 0)
    col = lax.broadcasted_iota(jnp.int32, bias.shape, 1)
    bias[...] = jnp.where(col <= row + half * rows, 0.0, -1e30)
    counted[...] = jnp.ones_like(counted)

    @pl.when(pair < 2)
    def _():
        for d in (2, 3, 4):

            @pl.when(2 * pair + 1 - d < 0)
            def _():
                counted[d] = jnp.zeros_like(counted[d])

    def attend(chunk):
        @pl.when(pair < 2)
        def _():
            seen = jnp.broadcast_to(kv[chunk, 0, 1, 0][:1], (rows, HEAD_SIZE))
            for d in (2, 3, 4):

                @pl.when(2 * pair + 1 - d < 0)
                def _():
                    kv[chunk, 0, d, 0] = seen
                    kv[chunk, 0, d, 1] = seen

        for side in range(2):
            first = 1 - side
            heads = [pl.ds(chunk * wide + head * HEAD_SIZE, HEAD_SIZE) for head in range(groups)]
            query = jnp.concatenate([q_here[side, :, cols] for cols in heads], axis=0)
            key = kv[chunk, 0, first : first + 4].reshape(keys, HEAD_SIZE)
            value = kv[chunk, 1, first : first + 4].reshape(keys, HEAD_SIZE)
            ones = counted[first : first + 4].reshape(keys, HEAD_SIZE)
            scores = lax.dot_general(
                query, key, (((1,), (1,)), ((), ())), preferred_element_type=jnp.float32
            )
            parts = []
            for head in range(groups):
                part = scores[head * rows : (head + 1) * rows]
                part = jnp.concatenate([part[:, : 2 * rows] + bias[...], part[:, 2 * rows :]], axis=1)
                top = jnp.max(part, axis=1, keepdims=True)
                parts.append(jnp.exp2((part - top) * factor).astype(jnp.bfloat16))
            mixed = jnp.dot(
                jnp.concatenate(parts, axis=0),
                jnp.concatenate([value, ones], axis=1),
                preferred_element_type=jnp.float32,
            )
            result = (mixed[:, :HEAD_SIZE] / mixed[:, HEAD_SIZE:]).astype(jnp.bfloat16)
            for head, cols in enumerate(heads):
                o_here[side, :, cols] = result[head * rows : (head + 1) * rows]

    outs = []

    def give(chunk):
        here = pl.ds(chunk * wide, wide)
        there = pl.ds(pl.multiple_of(core * q_cols + chunk * wide, wide), wide)
        copy = pltpu.make_async_copy(o_here.at[core, :, here], out_ref.at[:, there], o_sem.at[0, chunk])
        copy.start()
        outs.append(copy)
        send(
            o_here.at[1 - core, :, here],
            out_ref.at[:, there],
            o_sem.at[1, chunk],
            o_sem.at[2, chunk],
            mate,
            always,
        )

    def ask(_):
        send(q_part(q_ref, 1 - core), q_here.at[core], q_sem.at[1], q_sem.at[2], mate, always)

    def await_queries(_):
        q_own.wait()
        pltpu.make_async_copy(q_here.at[1 - core], q_here.at[1 - core], q_sem.at[2]).wait()

    def finish(chunk):
        gather(chunk)
        attend(chunk)
        give(chunk)

    for chunk in range(chunks + 2):
        if chunk < chunks:
            origin(chunk)
            if chunk == 0:
                ask(chunk)
        if 0 < chunk <= chunks:
            relay_first(chunk - 1)
            relay_cross(chunk - 1)
            relay_own(chunk - 1)
        if 1 < chunk:
            relay_other(chunk - 2)
            cross_last(chunk - 2)
            if chunk == 2:
                await_queries(chunk)
            if chunk > 2:
                finish(chunk - 3)
    finish(chunks - 1)
    for copy, exists in pending:

        @pl.when(exists)
        def _():
            copy.wait_send()

    for chunk in range(chunks):
        outs[chunk].wait()
        there = pl.ds(pl.multiple_of((1 - core) * q_cols + chunk * wide, wide), wide)
        ref = out_ref.at[:, there]
        pltpu.make_async_copy(ref, ref, o_sem.at[2, chunk]).wait()


def on_device_pairs(blocks, queries, keys, values):
    rows = queries.shape[0]
    kv_heads = keys.shape[1] // HEAD_SIZE
    groups = queries.shape[1] // keys.shape[1]
    chunks = kv_heads // 2
    dma = pltpu.SemaphoreType.DMA
    flops = 4 * rows * queries.shape[1] * 8 * rows
    queries, keys, values = (pltpu.with_memory_space_constraint(a, pltpu.HBM) for a in (queries, keys, values))
    return pl.pallas_call(
        functools.partial(attention_kernel, blocks // 2, groups),
        out_shape=jax.ShapeDtypeStruct(queries.shape, queries.dtype),
        in_specs=[pl.BlockSpec(memory_space=pltpu.HBM)] * 3,
        out_specs=pl.BlockSpec(memory_space=pl.ANY),
        scratch_shapes=[
            pltpu.VMEM((chunks, 2, 5, 2, rows, HEAD_SIZE), jnp.bfloat16),
            pltpu.VMEM((2, rows, queries.shape[1] // 2), jnp.bfloat16),
            pltpu.VMEM((2, rows, queries.shape[1] // 2), jnp.bfloat16),
            pltpu.VMEM((rows, 2 * rows), jnp.float32),
            pltpu.VMEM((5, 2, rows, HEAD_SIZE), jnp.bfloat16),
            dma((chunks, 2, 2)),
            dma((chunks, 2)),
            dma((chunks, 5, 2)),
            dma((chunks, 10)),
            dma((3,)),
            dma((3, chunks)),
        ],
        compiler_params=pltpu.CompilerParams(
            collective_id=0, has_side_effects=True, vmem_limit_bytes=32 * 2**20
        ),
        cost_estimate=pl.CostEstimate(flops=flops, bytes_accessed=6 * queries.size, transcendentals=flops // 512),
    )(queries, keys, values)


def solution(mesh):
    placed = (P(("ctx", "uly"), None), P(("ctx", "uly"), None), P(("ctx", "uly"), None))
    blocks, halves = mesh.shape["ctx"], mesh.shape["uly"]
    body = on_device
    if halves == 2 and blocks % 4 == 0:
        body = functools.partial(on_device_pairs, blocks)
    return jax.shard_map(
        body, mesh=mesh, in_specs=placed, out_specs=P(("ctx", "uly"), None), check_vma=False
    )
```
